32 devices in a mesh: py: 4 (over z), pz: 8 (over y, x, core).
Axes of the slice: x: 2, y: 2, z: 4, core: 2. Of those that a mesh axis runs over, the one named last changes fastest.
Arguments:
- vort_p: bfloat16 [3, 131072], P(None, ('py', 'pz')), may hold values from -6 to 6
- pair_weights: bfloat16 [8192, 64, 128], P(('py', 'pz')), may hold values from -1.796875 to 1.796875
- pair_part: int32 [8192], P(('py', 'pz')), may hold values from 0 to 31
- pair_node: int32 [8192], P(('py', 'pz')), may hold values from 0 to 95, as said below
- counts: int32 [32], P(('py', 'pz')), may hold values from 128 to 256, as said below
Outputs:
- vel_p: float32 [3, 131072], P(None, ('py', 'pz'))
The draws below stay inside these ranges and needn't reach their ends.
Inputs may be any that keep to these rules, and one draw needn't show every extreme that they name: `counts`: every pencil has at least 128 live slots, and some pencil has all 256 slots live in every draw. `pair_node`: in every pencil the slots below 96 name each of its node blocks exactly once.
All inputs are finite; a program needn't handle non-finite values.
Results may differ from the reference program's by a relative error of at most 0.0029.
Values sent between devices are 32-bit elements; how exact they have to be, the bound alone decides.
A program may use at most 64 MiB of HBM per device.

```python
import math
import jax
import jax.numpy as jnp
from jax import lax

NX = 384
CY = 8
CZ = 2
BP = 128
BN = 64
PB_DEV = 32
PAIR_DEV = 256
NB_DEV = 96
PENCILS = 32
PARTS_SIZE = 131072
PAIRS = 8192
NY = 32
NZ = 16
N_PY = 4
N_PZ = 8


def draw_counts(key, part):
    first, second, third = jax.random.split(key, 3)
    spread_top = PAIR_DEV - PAIR_DEV // 2
    draw_one = jax.random.randint(first, (PENCILS,), 0, spread_top + 1)
    draw_two = jax.random.randint(second, (PENCILS,), 0, spread_top + 1)
    base = PAIR_DEV // 2 + jnp.minimum(draw_one, draw_two)
    busiest = jax.random.randint(third, (), 0, PENCILS)
    return jnp.where(jnp.arange(PENCILS) == busiest, PAIR_DEV, base).astype(jnp.int32)


def draw_pair_node(key, part):
    order_key, rest_key = jax.random.split(jax.random.fold_in(key, 17))
    pencil_keys = jax.random.split(order_key, PENCILS)
    covering = jax.vmap(lambda one_key: jax.random.permutation(one_key, NB_DEV))(pencil_keys).astype(jnp.int32)
    others = jax.random.randint(rest_key, (PENCILS, PAIR_DEV - NB_DEV), 0, NB_DEV).astype(jnp.int32)
    return jnp.concatenate([covering, others], axis=1).reshape(PENCILS * PAIR_DEV)


def plant(drawn, own_key, least, high):
    extent = drawn.shape
    index_at = [jax.random.randint(jax.random.fold_in(own_key, axis), (), 0, extent[axis]) for axis in range(len(extent))]
    drawn = drawn.at[tuple(index_at)].set(least)
    longest = extent.index(max(extent))
    index_at[longest] = (index_at[longest] + 1) % extent[longest]
    return drawn.at[tuple(index_at)].set(high)


def levels(own_key, shape, cuts, least, top_value):
    loudness, own = 1.0, jax.random.fold_in(own_key, 6)
    for dim, blocks in cuts:
        heights = jnp.exp(jax.random.uniform(jax.random.fold_in(own, dim), (blocks,), jnp.float32, least / len(cuts), top_value / len(cuts)))
        loudness = loudness * jnp.repeat(heights, shape[dim] // blocks).reshape([-1 if axis == dim else 1 for axis in range(len(shape))])
    return loudness


def bell_draw(rng, shape, deviation, limit, pieces=(), dtype=jnp.bfloat16):
    result = jax.random.normal(rng, shape, jnp.float32) * deviation
    if len(pieces) > 0:
        result = levels(rng, shape, pieces, -0.22, 0.18) * result
    return jnp.clip(result, min=-limit, max=limit).astype(dtype)


def setup_inputs(seed: int = 0) -> dict:
    key_list = jax.random.split(jax.random.key(seed), 6)
    return {
        "vort_p": bell_draw(key_list[0], (3, PARTS_SIZE), 1.0, 6.0, ((1, 32),)),
        "pair_weights": bell_draw(key_list[1], (PAIRS, BN, BP), 0.3, 1.796875, ((0, 32),)),
        "pair_part": plant(jax.random.randint(key_list[2], (PAIRS,), 0, PB_DEV), jax.random.fold_in(key_list[2], 1), 0, PB_DEV - 1).astype(jnp.int32),
        "pair_node": draw_pair_node(jax.random.fold_in(key_list[5], 71), 0),
        "counts": draw_counts(jax.random.fold_in(key_list[5], 71), 0),
    }


def cross_terms(coeffs, field):
    return jnp.stack([coeffs[1] * field[2] - coeffs[2] * field[1], coeffs[2] * field[0] - coeffs[0] * field[2], coeffs[0] * field[1] - coeffs[1] * field[0]], axis=0)


def signed_wave(length, count):
    index = jnp.arange(count)
    signed = jnp.where(index < length // 2, index, index - length)
    return signed.astype(jnp.float32) * (2.0 * math.pi / length), index == length // 2


def reference(vort_p, pair_weights, pair_part, pair_node, counts):
    node_blocks = NX * CY * CZ // BN
    particle_blocks = vort_p.reshape(3, PENCILS, PB_DEV, BP).transpose(1, 2, 0, 3)
    tile_weights = pair_weights.reshape(PENCILS, PAIR_DEV, BN, BP)
    part_index = pair_part.reshape(PENCILS, PAIR_DEV)
    node_index = pair_node.reshape(PENCILS, PAIR_DEV)

    def spread(inputs):
        blocks, weights, parts, nodes, count = inputs
        picked = blocks[parts].astype(jnp.float32)
        products = jnp.einsum('pcq,pnq->pcn', picked, weights.astype(jnp.float32))
        live_mask = (jnp.arange(PAIR_DEV) < count).astype(jnp.float32)
        products = products * live_mask[:, None, None]
        return jax.ops.segment_sum(products, nodes, num_segments=node_blocks)

    local_nodes = lax.map(spread, (particle_blocks, tile_weights, part_index, node_index, counts))
    vort_grid = local_nodes.transpose(0, 2, 1, 3).reshape(N_PY, N_PZ, 3, CZ, CY, NX)
    vort_grid = vort_grid.transpose(2, 1, 3, 0, 4, 5).reshape(3, NZ, NY, NX)
    vort_hat = jnp.fft.rfftn(vort_grid, axes=(1, 2, 3))
    x_modes = NX // 2 + 1
    wave_z, edge_z = signed_wave(NZ, NZ)
    wave_y, edge_y = signed_wave(NY, NY)
    mode_x = jnp.arange(x_modes)
    wave_x = mode_x.astype(jnp.float32) * (2.0 * math.pi / NX)
    edge_x = mode_x == NX // 2
    wave_x3 = wave_x[None, None, :]
    wave_y3 = wave_y[None, :, None]
    wave_z3 = wave_z[:, None, None]
    total = wave_x3 * wave_x3 + wave_y3 * wave_y3 + wave_z3 * wave_z3
    edges = edge_z[:, None, None] | edge_y[None, :, None] | edge_x[None, None, :]
    keep = (total > 0) & jnp.logical_not(edges)
    inverse_sq = jnp.where(keep, 1.0 / jnp.where(keep, total, 1.0), 0.0)
    inv_wave = (wave_x3 * inverse_sq, wave_y3 * inverse_sq, wave_z3 * inverse_sq)
    vel_hat = 1j * cross_terms(inv_wave, vort_hat)
    vel_grid = jnp.fft.irfftn(vel_hat, s=(NZ, NY, NX), axes=(1, 2, 3)).astype(jnp.bfloat16)
    vel_nodes = vel_grid.reshape(3, N_PZ, CZ, N_PY, CY, NX).transpose(3, 1, 0, 2, 4, 5)
    vel_nodes = vel_nodes.reshape(PENCILS, 3, node_blocks, BN).transpose(0, 2, 1, 3)

    def collect(inputs):
        nodes_vel, weights, parts, nodes, count = inputs
        picked = nodes_vel[nodes].astype(jnp.float32)
        products = jnp.einsum('pcn,pnq->pcq', picked, weights.astype(jnp.float32))
        live_mask = (jnp.arange(PAIR_DEV) < count).astype(jnp.float32)
        products = products * live_mask[:, None, None]
        return jax.ops.segment_sum(products, parts, num_segments=PB_DEV)

    per_block = lax.map(collect, (vel_nodes, tile_weights, part_index, node_index, counts))
    return per_block.transpose(2, 0, 1, 3).reshape(3, PARTS_SIZE)
```

```python
import functools
import math

import jax
import jax.numpy as jnp
import numpy as np
from jax import lax
from jax.experimental import pallas as pl
from jax.experimental.pallas import tpu as pltpu
from jax.sharding import PartitionSpec as P

NX = 384
CY = 8
CZ = 2
BP = 128
BN = 64
PB_DEV = 32
ROWS = 8
CHUNK = 32
GROUP = 16
MESH = pl.DeviceIdType.MESH
f32 = jnp.float32
bf16 = jnp.bfloat16


def twiddle(row_index, col_index, period):
    product = row_index[:, None] * col_index[None, :] % period
    return product.astype(jnp.float32) * (2.0 * math.pi / period)


def forward_table(length):
    angle = twiddle(jnp.arange(length), jnp.arange(length), length)
    cosine = jnp.cos(angle)
    sines = jnp.sin(angle)
    return jnp.stack([jnp.stack([cosine, -sines], 1), jnp.stack([sines, cosine], 1)], 0)


def inverse_table(length):
    angle = twiddle(jnp.arange(length), jnp.arange(length), length)
    cosine = jnp.cos(angle) / length
    sines = jnp.sin(angle) / length
    return jnp.stack([jnp.stack([cosine, sines], 1), jnp.stack([-sines, cosine], 1)], 0)


def cross_terms(coeffs, field):
    return jnp.stack(
        [
            coeffs[1] * field[2] - coeffs[2] * field[1],
            coeffs[2] * field[0] - coeffs[0] * field[2],
            coeffs[0] * field[1] - coeffs[1] * field[0],
        ],
        axis=0,
    )


def signed_wave(length, index):
    signed = jnp.where(index < length // 2, index, index - length)
    return (signed.astype(jnp.float32) * (2.0 * math.pi / length), index == length // 2)


def curl_solve(spectrum, y_cells, z_cells):
    x_local = spectrum.shape[1]
    y_local = spectrum.shape[3]
    mode_x = lax.axis_index("py") * x_local + jnp.arange(x_local)
    wave_x = mode_x.astype(jnp.float32) * (2.0 * math.pi / NX)
    wave_y, edge_y = signed_wave(y_cells, lax.axis_index("pz") * y_local + jnp.arange(y_local))
    wave_z, edge_z = signed_wave(z_cells, jnp.arange(z_cells))
    wave_x3 = wave_x[:, None, None]
    wave_y3 = wave_y[None, :, None]
    wave_z3 = wave_z[None, None, :]
    total = wave_x3 * wave_x3 + wave_y3 * wave_y3 + wave_z3 * wave_z3
    edges = edge_y[None, :, None] | edge_z[None, None, :]
    keep = (total > 0) & jnp.logical_not(edges)
    inverse_sq = jnp.where(keep, 1.0 / jnp.where(keep, total, 1.0), 0.0)
    inv_wave = (wave_x3 * inverse_sq, wave_y3 * inverse_sq, wave_z3 * inverse_sq)
    real_turn = cross_terms(inv_wave, spectrum[:, :, 0])
    imag_turn = cross_terms(inv_wave, spectrum[:, :, 1])
    return jnp.stack([-imag_turn, real_turn], axis=2)


def halves(table):
    table = np.asarray(table, np.float32)
    high = table.astype(bf16)
    return high, (table - high.astype(np.float32)).astype(bf16)


def split(x):
    high = x.astype(bf16)
    return high, (x - high.astype(f32)).astype(bf16)


def dot(a, b, dims=((1,), (0,))):
    return lax.dot_general(a, b, (dims, ((), ())), preferred_element_type=f32)


def spread_kernel(part, node, count, parts_ref, w_ref, out_ref):
    step = pl.program_id(0)

    @pl.when(step == 0)
    def _():
        out_ref[...] = jnp.zeros_like(out_ref)

    def group(g, carry):
        sums = []
        for i in range(GROUP):
            p = g * GROUP + i
            slot = step * CHUNK + p
            start = pl.multiple_of(part[slot] * BP, BP)
            picked = parts_ref[:, pl.ds(start, BP)]
            got = dot(picked, w_ref[p], ((1,), (1,)))
            sums.append(jnp.where(slot < count[0], got, 0.0))
        for i in range(GROUP):
            j = node[step * CHUNK + g * GROUP + i]
            out_ref[j, 0:3, :] += sums[i]
        return carry

    lax.fori_loop(0, CHUNK // GROUP, group, 0)


def spread(vort_p, weights, part, node, counts, node_blocks):
    slots = weights.shape[0]
    return pl.pallas_call(
        spread_kernel,
        out_shape=jax.ShapeDtypeStruct((node_blocks, ROWS, BN), f32),
        grid_spec=pltpu.PrefetchScalarGridSpec(
            num_scalar_prefetch=3,
            grid=(slots // CHUNK,),
            in_specs=[
                pl.BlockSpec(vort_p.shape, lambda i, *_: (0, 0)),
                pl.BlockSpec((CHUNK, BN, BP), lambda i, *_: (i, 0, 0)),
            ],
            out_specs=pl.BlockSpec((node_blocks, ROWS, BN), lambda i, *_: (0, 0, 0)),
        ),
        name="spread",
    )(part, node, counts, vort_p, weights)


def collect_kernel(part, node, count, vel_ref, w_ref, out_ref, sums_ref):
    step = pl.program_id(0)

    @pl.when(step == 0)
    def _():
        sums_ref[...] = jnp.zeros_like(sums_ref)

    def group(g, carry):
        sums = []
        for i in range(GROUP):
            p = g * GROUP + i
            slot = step * CHUNK + p
            chosen = vel_ref[node[slot]].astype(bf16)
            got = dot(chosen, w_ref[p])
            sums.append(jnp.where(slot < count[0], got, 0.0))
        for i in range(GROUP):
            b = part[step * CHUNK + g * GROUP + i]
            sums_ref[b] += sums[i]
        return carry

    lax.fori_loop(0, CHUNK // GROUP, group, 0)

    @pl.when(step == pl.num_programs(0) - 1)
    def _():
        for b in range(PB_DEV):
            out_ref[:, b * BP : (b + 1) * BP] = sums_ref[b, 0:3, :]


def collect(vel, weights, part, node, counts):
    slots = weights.shape[0]
    return pl.pallas_call(
        collect_kernel,
        out_shape=jax.ShapeDtypeStruct((3, PB_DEV * BP), f32),
        grid_spec=pltpu.PrefetchScalarGridSpec(
            num_scalar_prefetch=3,
            grid=(slots // CHUNK,),
            in_specs=[
                pl.BlockSpec(vel.shape, lambda i, *_: (0, 0, 0)),
                pl.BlockSpec((CHUNK, BN, BP), lambda i, *_: (i, 0, 0)),
            ],
            out_specs=pl.BlockSpec((3, PB_DEV * BP), lambda i, *_: (0, 0)),
            scratch_shapes=[pltpu.VMEM((PB_DEV, ROWS, BP), f32)],
        ),
        name="collect",
    )(part, node, counts, vel, weights)


def tables(n_py, n_pz):
    devices = n_py * n_pz
    local = NX // 2 // devices
    ny, nz = CY * n_py, CZ * n_pz
    row = np.arange(devices * ROWS)
    slot, device = row % ROWS, row // ROWS
    mode = device * local + slot
    angle = 2 * np.pi * (mode[:, None] * np.arange(NX)[None] % NX) / NX
    used = (slot < local)[:, None]
    x_cos, x_sin = np.where(used, np.cos(angle), 0.0), np.where(used, -np.sin(angle), 0.0)
    index = np.arange(devices)
    a, b = index // n_pz, index % n_pz
    theta = 2 * np.pi * (a[:, None] * a[None] / n_py + b[:, None] * b[None] / n_pz)
    eye = np.eye(ROWS)
    far = np.concatenate([np.kron(np.cos(theta), eye), np.kron(np.sin(theta), eye)], 0)
    lane = np.arange(128)
    real, comp, cell = lane // 64, lane % 64 // 16, lane % 16
    zl, yl = cell // CY, cell % CY
    valid = (comp < 3)[None]
    phi = 2 * np.pi * (a[:, None] * yl[None] / ny + b[:, None] * zl[None] / nz)
    sign = np.where(real == 0, 1.0, -1.0)[None]
    turn_cos, turn_sin = np.cos(phi), np.sin(phi) * sign
    psi = 2 * np.pi * (yl[:, None] * yl[None] / CY + zl[:, None] * zl[None] / CZ)

    def near(ahead):
        cosine, sines = np.cos(psi), np.sin(psi)
        r, q = real[:, None], real[None]
        both = np.where(r == q, sines, np.where(r == 0, cosine, -cosine))
        same = (comp[:, None] == (comp[None] + ahead) % 3) & (comp[:, None] < 3) & valid
        return np.where(same, both, 0.0)

    forward = np.concatenate([near(2), near(1)], 1)
    cosine, sines = np.cos(psi), np.sin(psi)
    r, q = real[:, None], real[None]
    both = np.where(r == q, cosine, np.where(r == 0, sines, -sines))
    same = (comp[:, None] == comp[None]) & (comp[:, None] < 3)
    back = np.where(same, both, 0.0)
    my, mz = a[:, None] + n_py * yl[None], b[:, None] + n_pz * zl[None]
    keep = (my != ny // 2) & (mz != nz // 2) & valid
    my, mz = np.where(my < ny // 2, my, my - ny), np.where(mz < nz // 2, mz, mz - nz)
    ky, kz = 2 * np.pi * my / ny, 2 * np.pi * mz / nz
    zero = np.zeros_like(ky)
    wave = np.stack([zero, ky, kz])
    k_first = np.where(comp == 0, wave[1], np.where(comp == 1, wave[2], wave[0]))
    k_second = np.where(comp == 0, wave[2], np.where(comp == 1, wave[0], wave[1]))
    x_first = np.broadcast_to(comp == 2, ky.shape)
    x_second = np.broadcast_to(comp == 1, ky.shape)
    small = [turn_cos, turn_sin, ky * ky + kz * kz, k_first, k_second, x_first, x_second, keep]
    small = np.stack(small).astype(np.float32)
    return [
        *halves(np.stack([x_cos, x_sin])),
        *halves(far),
        *halves(forward),
        *halves(back),
        small,
    ]


def solve_kernel(
    n_py,
    n_pz,
    grid_ref,
    xh_ref,
    xl_ref,
    far_h,
    far_l,
    fwd_h,
    fwd_l,
    back_h,
    back_l,
    small,
    out_ref,
    send_a,
    recv_a,
    send_b,
    recv_b,
    send_sem,
    recv_sem,
):
    devices = n_py * n_pz
    local = NX // 2 // devices
    rows = devices * ROWS
    per_row = NX // BN
    cells = CY * CZ
    me = lax.axis_index("py") * n_pz + lax.axis_index("pz")
    barrier = pltpu.get_barrier_semaphore()

    def greet(k, carry):
        other = lax.rem(me + k, devices)
        pl.semaphore_signal(
            barrier, inc=1, device_id=(other // n_pz, lax.rem(other, n_pz)), device_id_type=MESH
        )
        return carry

    lax.fori_loop(1, devices, greet, 0)

    def exchange(send, recv, phase):
        def copy(k, carry):
            other = lax.rem(me + k, devices)
            pltpu.make_async_remote_copy(
                src_ref=send.at[other],
                dst_ref=recv.at[me],
                send_sem=send_sem.at[phase],
                recv_sem=recv_sem.at[phase],
                device_id=(other // n_pz, lax.rem(other, n_pz)),
                device_id_type=MESH,
            ).start()
            return carry

        lax.fori_loop(1, devices, copy, 0)

    def finish(send, recv, phase):
        many = pl.ds(0, devices - 1)
        pltpu.make_async_copy(recv.at[many], recv.at[many], recv_sem.at[phase]).wait()

    def drain(send, phase):
        many = pl.ds(0, devices - 1)
        pltpu.make_async_copy(send.at[many], send.at[many], send_sem.at[phase]).wait()

    lines = []
    for c in range(3):
        pieces = [
            grid_ref[pl.ds(xb * ROWS + c, cells, stride=per_row * ROWS), :]
            for xb in range(per_row)
        ]
        lines.append(jnp.concatenate(pieces, axis=1))
    vort = jnp.concatenate(lines, axis=0)
    low = jnp.concatenate([vort, jnp.zeros((80, NX), f32)], axis=0)
    up = jnp.concatenate([jnp.zeros((64, NX), f32), vort, jnp.zeros((16, NX), f32)], axis=0)
    over = ((1,), (1,))
    modes = jnp.zeros((rows, 128), f32)
    for k, field in ((0, low), (1, up)):
        high, rest = split(field)
        modes += dot(xh_ref[k], high, over) + (
            dot(xh_ref[k], rest, over) + dot(xl_ref[k], high, over)
        )
    send_a[...] = modes.reshape(devices, ROWS, 128)
    recv_a[me] = send_a[me]
    pl.semaphore_wait(barrier, devices - 1)
    exchange(send_a, recv_a, 0)

    def spread_out(i):
        return jnp.broadcast_to(small[i][:, None, :], (devices, ROWS, 128)).reshape(rows, 128)

    slot = lax.broadcasted_iota(jnp.int32, (rows, 128), 0) % ROWS
    mode = me * local + slot
    wave_x = mode.astype(f32) * (2.0 * math.pi / NX)
    total = spread_out(2) + wave_x * wave_x
    ny_nz = CY * n_py * CZ * n_pz
    weight = jnp.where(mode == 0, 1.0, 2.0) * (1.0 / (NX * ny_nz))
    inverse = spread_out(7) * weight / jnp.where(total > 0, total, 1.0)
    gain_a = (spread_out(3) + wave_x * spread_out(5)) * inverse
    gain_b = (spread_out(4) + wave_x * spread_out(6)) * inverse
    turn_cos, turn_sin = spread_out(0), spread_out(1)
    sign = jnp.where(lax.broadcasted_iota(jnp.int32, (rows, 128), 1) < 64, 1.0, -1.0)

    def swap(x):
        return pltpu.roll(x, 64, 1)

    def across(x):
        high, rest = split(x)
        both = dot(far_h[...], high) + (dot(far_h[...], rest) + dot(far_l[...], high))
        return both[:rows], swap(both[rows:]) * sign

    def along(x, table_h, table_l):
        high, rest = split(x)
        return dot(high, table_h[...]) + (dot(rest, table_h[...]) + dot(high, table_l[...]))

    finish(send_a, recv_a, 0)
    even, odd = across(recv_a[...].reshape(rows, 128))
    y = even + odd
    z = turn_cos * y + turn_sin * swap(y)
    both = along(z, fwd_h, fwd_l)
    vel = gain_a * both[:, :128] - gain_b * both[:, 128:]
    y = along(vel, back_h, back_l)
    z = turn_cos * y - turn_sin * swap(y)
    even, odd = across(z)
    send_b[...] = (even - odd).reshape(devices, ROWS, 128)
    recv_b[me] = send_b[me]
    exchange(send_b, recv_b, 1)
    drain(send_a, 0)
    finish(send_b, recv_b, 1)
    back = recv_b[...].reshape(rows, 128).T
    grid = jnp.zeros((48, NX), f32)
    for k in range(2):
        high, rest = split(back[64 * k : 64 * k + 48])
        grid += dot(high, xh_ref[k]) + (dot(rest, xh_ref[k]) + dot(high, xl_ref[k]))
    grid = grid.astype(bf16).astype(f32)
    for c in range(3):
        for xb in range(per_row):
            out_ref[pl.ds(xb * ROWS + c, cells, stride=per_row * ROWS), :] = grid[
                c * cells : (c + 1) * cells, xb * BN : (xb + 1) * BN
            ]
    drain(send_b, 1)


def solve_direct(sums, n_py, n_pz):
    devices = n_py * n_pz
    vmem = pl.BlockSpec(memory_space=pltpu.VMEM)
    block = pltpu.VMEM((devices, ROWS, 128), f32)
    consts = tables(n_py, n_pz)
    flat = sums.reshape(-1, BN)
    out = pl.pallas_call(
        functools.partial(solve_kernel, n_py, n_pz),
        out_shape=jax.ShapeDtypeStruct(flat.shape, f32),
        in_specs=[vmem] * (1 + len(consts)),
        out_specs=vmem,
        scratch_shapes=[
            block,
            block,
            block,
            block,
            pltpu.SemaphoreType.DMA((2,)),
            pltpu.SemaphoreType.DMA((2,)),
        ],
        compiler_params=pltpu.CompilerParams(
            collective_id=0, has_side_effects=True, vmem_limit_bytes=32 * 2**20
        ),
        name="solve",
    )(flat, *[jnp.asarray(t) for t in consts])
    return out.reshape(sums.shape)


def solve_staged(sums, n_py, n_pz):
    highest = lax.Precision.HIGHEST
    node_blocks = sums.shape[0]
    y_cells, z_cells = CY * n_py, CZ * n_pz
    x_modes = NX // 2
    vort_grid = sums[:, :3].transpose(1, 0, 2).reshape(3, CZ, CY, NX)
    angle_fwd = twiddle(jnp.arange(NX), jnp.arange(x_modes), NX)
    x_forward = jnp.stack([jnp.cos(angle_fwd), -jnp.sin(angle_fwd)], 1)
    angle_inv = twiddle(jnp.arange(x_modes), jnp.arange(NX), NX)
    mode_weight = (jnp.where(jnp.arange(x_modes) == 0, 1.0, 2.0) / NX)[:, None]
    x_inverse = jnp.stack([mode_weight * jnp.cos(angle_inv), -mode_weight * jnp.sin(angle_inv)], 0)
    y_forward = forward_table(y_cells)
    z_forward = forward_table(z_cells)
    z_inverse = inverse_table(z_cells)
    y_inverse = inverse_table(y_cells)
    x_spectrum = jnp.einsum("czyx,xrm->czrmy", vort_grid, x_forward, precision=highest)
    row_section = jnp.einsum(
        "czrmy,rysk->cmskz",
        lax.all_to_all(x_spectrum, "py", split_axis=3, concat_axis=4, tiled=True),
        y_forward,
        precision=highest,
    )
    col_section = jnp.einsum(
        "cmrkz,rzsw->cmskw",
        lax.all_to_all(row_section, "pz", split_axis=3, concat_axis=4, tiled=True),
        z_forward,
        precision=highest,
    )
    vel_spectrum = curl_solve(col_section, y_cells, z_cells)
    z_back = jnp.einsum("cmrkw,rwsz->cmszk", vel_spectrum, z_inverse, precision=highest)
    y_back = jnp.einsum(
        "cmrzk,rksy->czsym",
        lax.all_to_all(z_back, "pz", split_axis=3, concat_axis=4, tiled=True),
        y_inverse,
        precision=highest,
    )
    vel_grid = jnp.einsum(
        "czrym,rmx->czyx",
        lax.all_to_all(y_back, "py", split_axis=3, concat_axis=4, tiled=True),
        x_inverse,
        precision=highest,
    )
    vel_nodes = vel_grid.astype(bf16).astype(f32).reshape(3, node_blocks, BN).transpose(1, 0, 2)
    return jnp.pad(vel_nodes, ((0, 0), (0, ROWS - 3), (0, 0)))


def per_device(vort_p, pair_weights, pair_part, pair_node, counts):
    n_py, n_pz = lax.axis_size("py"), lax.axis_size("pz")
    node_blocks = NX * CY * CZ // BN
    sums = spread(vort_p, pair_weights, pair_part, pair_node, counts, node_blocks)
    x_modes = NX // 2
    devices = n_py * n_pz
    direct = devices <= 32 and x_modes % devices == 0 and x_modes // devices <= ROWS
    vel = (solve_direct if direct else solve_staged)(sums, n_py, n_pz)
    return collect(vel, pair_weights, pair_part, pair_node, counts)


def solution(mesh):
    placed = (
        P(None, ("py", "pz")),
        P(("py", "pz"), None, None),
        P(("py", "pz")),
        P(("py", "pz")),
        P(("py", "pz")),
    )
    return jax.shard_map(
        per_device, mesh=mesh, in_specs=placed, out_specs=P(None, ("py", "pz")), check_vma=False
    )
```

```python
import functools
import math

import jax
import jax.numpy as jnp
import numpy as np
from jax import lax
from jax.experimental import pallas as pl
from jax.experimental.pallas import tpu as pltpu
from jax.sharding import PartitionSpec as P

NX = 384
CY = 8
CZ = 2
BP = 128
BN = 64
PB_DEV = 32
ROWS = 8
CHUNK = 32
GROUP = 4
MESH = pl.DeviceIdType.MESH
f32 = jnp.float32
bf16 = jnp.bfloat16


def twiddle(row_index, col_index, period):
    product = row_index[:, None] * col_index[None, :] % period
    return product.astype(jnp.float32) * (2.0 * math.pi / period)


def forward_table(length):
    angle = twiddle(jnp.arange(length), jnp.arange(length), length)
    cosine = jnp.cos(angle)
    sines = jnp.sin(angle)
    return jnp.stack([jnp.stack([cosine, -sines], 1), jnp.stack([sines, cosine], 1)], 0)


def inverse_table(length):
    angle = twiddle(jnp.arange(length), jnp.arange(length), length)
    cosine = jnp.cos(angle) / length
    sines = jnp.sin(angle) / length
    return jnp.stack([jnp.stack([cosine, sines], 1), jnp.stack([-sines, cosine], 1)], 0)


def cross_terms(coeffs, field):
    return jnp.stack(
        [
            coeffs[1] * field[2] - coeffs[2] * field[1],
            coeffs[2] * field[0] - coeffs[0] * field[2],
            coeffs[0] * field[1] - coeffs[1] * field[0],
        ],
        axis=0,
    )


def signed_wave(length, index):
    signed = jnp.where(index < length // 2, index, index - length)
    return (signed.astype(jnp.float32) * (2.0 * math.pi / length), index == length // 2)


def curl_solve(spectrum, y_cells, z_cells):
    x_local = spectrum.shape[1]
    y_local = spectrum.shape[3]
    mode_x = lax.axis_index("py") * x_local + jnp.arange(x_local)
    wave_x = mode_x.astype(jnp.float32) * (2.0 * math.pi / NX)
    wave_y, edge_y = signed_wave(y_cells, lax.axis_index("pz") * y_local + jnp.arange(y_local))
    wave_z, edge_z = signed_wave(z_cells, jnp.arange(z_cells))
    wave_x3 = wave_x[:, None, None]
    wave_y3 = wave_y[None, :, None]
    wave_z3 = wave_z[None, None, :]
    total = wave_x3 * wave_x3 + wave_y3 * wave_y3 + wave_z3 * wave_z3
    edges = edge_y[None, :, None] | edge_z[None, None, :]
    keep = (total > 0) & jnp.logical_not(edges)
    inverse_sq = jnp.where(keep, 1.0 / jnp.where(keep, total, 1.0), 0.0)
    inv_wave = (wave_x3 * inverse_sq, wave_y3 * inverse_sq, wave_z3 * inverse_sq)
    real_turn = cross_terms(inv_wave, spectrum[:, :, 0])
    imag_turn = cross_terms(inv_wave, spectrum[:, :, 1])
    return jnp.stack([-imag_turn, real_turn], axis=2)


def halves(table):
    table = np.asarray(table, np.float32)
    high = table.astype(bf16)
    return high, (table - high.astype(np.float32)).astype(bf16)


def split(x):
    high = x.astype(bf16)
    return high, (x - high.astype(f32)).astype(bf16)


def dot(a, b, dims=((1,), (0,))):
    return lax.dot_general(a, b, (dims, ((), ())), preferred_element_type=f32)


def left_half(shape):
    return lax.broadcasted_iota(jnp.int32, shape, 1) < BN


def spread_kernel(part, node, count, parts_ref, w_ref, out_ref, near_ref, parts, sems):
    chunks = w_ref.shape[0] // CHUNK

    def fetch(k):
        here = pl.ds(k * CHUNK, CHUNK)
        return pltpu.make_async_copy(w_ref.at[here], near_ref.at[here], sems.at[k])

    for k in range(chunks):
        fetch(k).start()
    out_ref[...] = jnp.zeros_like(out_ref)
    parts[...] = jnp.zeros_like(parts)
    for b in range(PB_DEV):
        parts[b, 0:3, :] = parts_ref[:, b * BP : (b + 1) * BP].astype(f32)
    left = left_half((ROWS, 128))

    def chunk(k, carry):
        fetch(k).wait()
        base = k * CHUNK
        for g in range(CHUNK // GROUP):
            first = base + g * GROUP
            picked = jnp.concatenate([parts[part[first + i]] for i in range(GROUP)], axis=0)
            tiles = near_ref[pl.ds(first, GROUP)].reshape(GROUP * BN, BP)
            got = dot(picked.astype(bf16), tiles, ((1,), (1,)))
            for i in range(GROUP):
                keep = jnp.logical_and(left if i % 2 == 0 else ~left, first + i < count[0])
                lanes = i // 2 * 128
                own = got[i * ROWS : (i + 1) * ROWS, lanes : lanes + 128]
                out_ref[node[first + i]] += jnp.where(keep, own, 0.0)
        return carry

    lax.fori_loop(0, chunks, chunk, 0)


def spread(vort_p, weights, part, node, counts, node_blocks):
    smem = pl.BlockSpec(memory_space=pltpu.SMEM)
    vmem = pl.BlockSpec(memory_space=pltpu.VMEM)
    return pl.pallas_call(
        spread_kernel,
        out_shape=(
            jax.ShapeDtypeStruct((node_blocks, ROWS, 2 * BN), f32),
            jax.ShapeDtypeStruct(weights.shape, weights.dtype),
        ),
        in_specs=[smem, smem, smem, vmem, pl.BlockSpec(memory_space=pltpu.HBM)],
        out_specs=(vmem, vmem),
        scratch_shapes=[
            pltpu.VMEM((PB_DEV, ROWS, BP), f32),
            pltpu.SemaphoreType.DMA((weights.shape[0] // CHUNK,)),
        ],
        compiler_params=pltpu.CompilerParams(vmem_limit_bytes=48 * 2**20),
        name="spread",
    )(part, node, counts, vort_p, weights)


def collect_kernel(part, node, count, vel_ref, w_ref, out_ref, sums):
    sums[...] = jnp.zeros_like(sums)
    left = left_half((ROWS, 128))
    zero = jnp.zeros((ROWS, 128), f32)

    def chunk(k, carry):
        for g in range(CHUNK // GROUP):
            first = k * CHUNK + g * GROUP
            rows = []
            for i in range(GROUP):
                slot = first + i
                keep = jnp.logical_and(left if i % 2 == 0 else ~left, slot < count[0])
                own = jnp.where(keep, vel_ref[node[slot]], 0.0)
                rows.append(
                    jnp.concatenate(
                        [own if h == i // 2 else zero for h in range(GROUP // 2)], axis=1
                    )
                )
            chosen = jnp.concatenate(rows, axis=0).astype(bf16)
            got = dot(chosen, w_ref[pl.ds(first, GROUP)].reshape(GROUP * BN, BP))
            for i in range(GROUP):
                sums[part[first + i]] += got[i * ROWS : (i + 1) * ROWS]
        return carry

    lax.fori_loop(0, w_ref.shape[0] // CHUNK, chunk, 0)
    for b in range(PB_DEV):
        out_ref[:, b * BP : (b + 1) * BP] = sums[b, 0:3, :]


def collect(vel, weights, part, node, counts):
    smem = pl.BlockSpec(memory_space=pltpu.SMEM)
    vmem = pl.BlockSpec(memory_space=pltpu.VMEM)
    return pl.pallas_call(
        collect_kernel,
        out_shape=jax.ShapeDtypeStruct((3, PB_DEV * BP), f32),
        in_specs=[smem, smem, smem, vmem, vmem],
        out_specs=vmem,
        scratch_shapes=[pltpu.VMEM((PB_DEV, ROWS, BP), f32)],
        compiler_params=pltpu.CompilerParams(vmem_limit_bytes=24 * 2**20),
        name="collect",
    )(part, node, counts, vel, weights)


def tables(n_py, n_pz):
    devices = n_py * n_pz
    local = NX // 2 // devices
    ny, nz = CY * n_py, CZ * n_pz
    row = np.arange(devices * ROWS)
    slot, device = row % ROWS, row // ROWS
    mode = device * local + slot
    angle = 2 * np.pi * (mode[:, None] * np.arange(NX)[None] % NX) / NX
    used = (slot < local)[:, None]
    x_cos, x_sin = np.where(used, np.cos(angle), 0.0), np.where(used, -np.sin(angle), 0.0)
    index = np.arange(devices)
    a, b = index // n_pz, index % n_pz
    theta = 2 * np.pi * (a[:, None] * a[None] / n_py + b[:, None] * b[None] / n_pz)
    eye = np.eye(ROWS)
    far = np.concatenate([np.kron(np.cos(theta), eye), np.kron(np.sin(theta), eye)], 0)
    lane = np.arange(128)
    real, comp, cell = lane // 64, lane % 64 // 16, lane % 16
    zl, yl = cell // CY, cell % CY
    valid = (comp < 3)[None]
    phi = 2 * np.pi * (a[:, None] * yl[None] / ny + b[:, None] * zl[None] / nz)
    sign = np.where(real == 0, 1.0, -1.0)[None]
    turn_cos, turn_sin = np.cos(phi), np.sin(phi) * sign
    psi = 2 * np.pi * (yl[:, None] * yl[None] / CY + zl[:, None] * zl[None] / CZ)

    def near(ahead):
        cosine, sines = np.cos(psi), np.sin(psi)
        r, q = real[:, None], real[None]
        both = np.where(r == q, sines, np.where(r == 0, cosine, -cosine))
        same = (comp[:, None] == (comp[None] + ahead) % 3) & (comp[:, None] < 3) & valid
        return np.where(same, both, 0.0)

    forward = np.concatenate([near(2), near(1)], 1)
    cosine, sines = np.cos(psi), np.sin(psi)
    r, q = real[:, None], real[None]
    both = np.where(r == q, cosine, np.where(r == 0, sines, -sines))
    same = (comp[:, None] == comp[None]) & (comp[:, None] < 3)
    back = np.where(same, both, 0.0)
    my, mz = a[:, None] + n_py * yl[None], b[:, None] + n_pz * zl[None]
    keep = (my != ny // 2) & (mz != nz // 2) & valid
    my, mz = np.where(my < ny // 2, my, my - ny), np.where(mz < nz // 2, mz, mz - nz)
    ky, kz = 2 * np.pi * my / ny, 2 * np.pi * mz / nz
    zero = np.zeros_like(ky)
    wave = np.stack([zero, ky, kz])
    k_first = np.where(comp == 0, wave[1], np.where(comp == 1, wave[2], wave[0]))
    k_second = np.where(comp == 0, wave[2], np.where(comp == 1, wave[0], wave[1]))
    x_first = np.broadcast_to(comp == 2, ky.shape)
    x_second = np.broadcast_to(comp == 1, ky.shape)
    small = [turn_cos, turn_sin, ky * ky + kz * kz, k_first, k_second, x_first, x_second, keep]
    small = np.stack(small).astype(np.float32)
    return [
        *halves(np.stack([x_cos, x_sin])),
        *halves(far),
        *halves(forward),
        *halves(back),
        small,
    ]


def solve_kernel(
    n_py,
    n_pz,
    grid_ref,
    xh_ref,
    xl_ref,
    far_h,
    far_l,
    fwd_h,
    fwd_l,
    back_h,
    back_l,
    small,
    out_ref,
    send_a,
    recv_a,
    send_b,
    recv_b,
    send_sem,
    recv_sem,
):
    devices = n_py * n_pz
    local = NX // 2 // devices
    rows = devices * ROWS
    per_row = NX // BN
    cells = CY * CZ
    my_y, my_z = lax.axis_index("py"), lax.axis_index("pz")
    me = my_y * n_pz + my_z
    barrier = pltpu.get_barrier_semaphore()
    recv_a[...] = jnp.zeros_like(recv_a)
    recv_b[...] = jnp.zeros_like(recv_b)

    def greet(k, carry):
        other = lax.rem(me + k, devices)
        pl.semaphore_signal(
            barrier, inc=1, device_id=(other // n_pz, lax.rem(other, n_pz)), device_id_type=MESH
        )
        return carry

    lax.fori_loop(1, devices, greet, 0)

    sent = pl.ds(0, local)

    def exchange(send, recv, phase):
        for k in range(1, devices):
            to_y = lax.rem(my_y + k // n_pz, n_py)
            to_z = lax.rem(my_z + k % n_pz, n_pz)
            pltpu.make_async_remote_copy(
                src_ref=send.at[to_y * n_pz + to_z, sent],
                dst_ref=recv.at[me, sent],
                send_sem=send_sem.at[phase],
                recv_sem=recv_sem.at[phase],
                device_id=(to_y, to_z),
                device_id_type=MESH,
            ).start()

    def finish(send, recv, phase):
        many = pl.ds(0, devices - 1)
        pltpu.make_async_copy(recv.at[many, sent], recv.at[many, sent], recv_sem.at[phase]).wait()

    def drain(send, phase):
        many = pl.ds(0, devices - 1)
        pltpu.make_async_copy(send.at[many, sent], send.at[many, sent], send_sem.at[phase]).wait()

    left = left_half((cells, 128))
    lines = []
    for c in range(3):
        pieces = []
        for xb in range(0, per_row, 2):
            first, second = (
                grid_ref[pl.ds((xb + h) * ROWS + c, cells, stride=per_row * ROWS), :]
                for h in (0, 1)
            )
            first += pltpu.roll(first, BN, 1)
            second += pltpu.roll(second, BN, 1)
            pieces.append(jnp.where(left, first, second))
        lines.append(jnp.concatenate(pieces, axis=1))
    vort = jnp.concatenate(lines, axis=0)
    low = jnp.concatenate([vort, jnp.zeros((80, NX), f32)], axis=0)
    up = jnp.concatenate([jnp.zeros((64, NX), f32), vort, jnp.zeros((16, NX), f32)], axis=0)
    over = ((1,), (1,))
    modes = jnp.zeros((rows, 128), f32)
    for k, field in ((0, low), (1, up)):
        high, rest = split(field)
        modes += dot(xh_ref[k], high, over) + (
            dot(xh_ref[k], rest, over) + dot(xl_ref[k], high, over)
        )
    send_a[...] = modes.reshape(devices, ROWS, 128)
    recv_a[me] = send_a[me]
    pl.semaphore_wait(barrier, devices - 1)
    exchange(send_a, recv_a, 0)

    def spread_out(i):
        return jnp.broadcast_to(small[i][:, None, :], (devices, ROWS, 128)).reshape(rows, 128)

    slot = lax.broadcasted_iota(jnp.int32, (rows, 128), 0) % ROWS
    mode = me * local + slot
    wave_x = mode.astype(f32) * (2.0 * math.pi / NX)
    total = spread_out(2) + wave_x * wave_x
    ny_nz = CY * n_py * CZ * n_pz
    weight = jnp.where(mode == 0, 1.0, 2.0) * (1.0 / (NX * ny_nz))
    inverse = spread_out(7) * weight / jnp.where(total > 0, total, 1.0)
    gain_a = (spread_out(3) + wave_x * spread_out(5)) * inverse
    gain_b = (spread_out(4) + wave_x * spread_out(6)) * inverse
    turn_cos, turn_sin = spread_out(0), spread_out(1)
    sign = jnp.where(lax.broadcasted_iota(jnp.int32, (rows, 128), 1) < 64, 1.0, -1.0)

    def swap(x):
        return pltpu.roll(x, 64, 1)

    def across(x):
        high, rest = split(x)
        both = dot(far_h[...], high) + (dot(far_h[...], rest) + dot(far_l[...], high))
        return both[:rows], swap(both[rows:]) * sign

    def along(x, table_h, table_l):
        high, rest = split(x)
        return dot(high, table_h[...]) + (dot(rest, table_h[...]) + dot(high, table_l[...]))

    finish(send_a, recv_a, 0)
    even, odd = across(recv_a[...].reshape(rows, 128))
    y = even + odd
    z = turn_cos * y + turn_sin * swap(y)
    both = along(z, fwd_h, fwd_l)
    vel = gain_a * both[:, :128] - gain_b * both[:, 128:]
    y = along(vel, back_h, back_l)
    z = turn_cos * y - turn_sin * swap(y)
    even, odd = across(z)
    send_b[...] = (even - odd).reshape(devices, ROWS, 128)
    recv_b[me] = send_b[me]
    exchange(send_b, recv_b, 1)
    drain(send_a, 0)
    finish(send_b, recv_b, 1)
    back = recv_b[...].reshape(rows, 128).T
    grid = jnp.zeros((48, NX), f32)
    for k in range(2):
        high, rest = split(back[64 * k : 64 * k + 48])
        grid += dot(high, xh_ref[k]) + (dot(rest, xh_ref[k]) + dot(high, xl_ref[k]))
    grid = grid.astype(bf16).astype(f32)
    for c in range(3):
        for xb in range(0, per_row, 2):
            piece = grid[c * cells : (c + 1) * cells, xb * BN : (xb + 2) * BN]
            other = pltpu.roll(piece, BN, 1)
            for h, both in ((0, jnp.where(left, piece, other)), (1, jnp.where(left, other, piece))):
                where = pl.ds((xb + h) * ROWS + c, cells, stride=per_row * ROWS)
                out_ref[where, :] = both
    drain(send_b, 1)


def solve_direct(sums, n_py, n_pz):
    devices = n_py * n_pz
    vmem = pl.BlockSpec(memory_space=pltpu.VMEM)
    block = pltpu.VMEM((devices, ROWS, 128), f32)
    consts = tables(n_py, n_pz)
    flat = sums.reshape(-1, 2 * BN)
    out = pl.pallas_call(
        functools.partial(solve_kernel, n_py, n_pz),
        out_shape=jax.ShapeDtypeStruct(flat.shape, f32),
        in_specs=[vmem] * (1 + len(consts)),
        out_specs=vmem,
        scratch_shapes=[
            block,
            block,
            block,
            block,
            pltpu.SemaphoreType.DMA((2,)),
            pltpu.SemaphoreType.DMA((2,)),
        ],
        compiler_params=pltpu.CompilerParams(
            collective_id=0, has_side_effects=True, vmem_limit_bytes=32 * 2**20
        ),
        name="solve",
    )(flat, *[jnp.asarray(t) for t in consts])
    return out.reshape(sums.shape)


def solve_staged(sums, n_py, n_pz):
    highest = lax.Precision.HIGHEST
    node_blocks = sums.shape[0]
    y_cells, z_cells = CY * n_py, CZ * n_pz
    x_modes = NX // 2
    sums = sums[:, :3, :BN] + sums[:, :3, BN:]
    vort_grid = sums.transpose(1, 0, 2).reshape(3, CZ, CY, NX)
    angle_fwd = twiddle(jnp.arange(NX), jnp.arange(x_modes), NX)
    x_forward = jnp.stack([jnp.cos(angle_fwd), -jnp.sin(angle_fwd)], 1)
    angle_inv = twiddle(jnp.arange(x_modes), jnp.arange(NX), NX)
    mode_weight = (jnp.where(jnp.arange(x_modes) == 0, 1.0, 2.0) / NX)[:, None]
    x_inverse = jnp.stack([mode_weight * jnp.cos(angle_inv), -mode_weight * jnp.sin(angle_inv)], 0)
    y_forward = forward_table(y_cells)
    z_forward = forward_table(z_cells)
    z_inverse = inverse_table(z_cells)
    y_inverse = inverse_table(y_cells)
    x_spectrum = jnp.einsum("czyx,xrm->czrmy", vort_grid, x_forward, precision=highest)
    row_section = jnp.einsum(
        "czrmy,rysk->cmskz",
        lax.all_to_all(x_spectrum, "py", split_axis=3, concat_axis=4, tiled=True),
        y_forward,
        precision=highest,
    )
    col_section = jnp.einsum(
        "cmrkz,rzsw->cmskw",
        lax.all_to_all(row_section, "pz", split_axis=3, concat_axis=4, tiled=True),
        z_forward,
        precision=highest,
    )
    vel_spectrum = curl_solve(col_section, y_cells, z_cells)
    z_back = jnp.einsum("cmrkw,rwsz->cmszk", vel_spectrum, z_inverse, precision=highest)
    y_back = jnp.einsum(
        "cmrzk,rksy->czsym",
        lax.all_to_all(z_back, "pz", split_axis=3, concat_axis=4, tiled=True),
        y_inverse,
        precision=highest,
    )
    vel_grid = jnp.einsum(
        "czrym,rmx->czyx",
        lax.all_to_all(y_back, "py", split_axis=3, concat_axis=4, tiled=True),
        x_inverse,
        precision=highest,
    )
    vel_nodes = vel_grid.astype(bf16).astype(f32).reshape(3, node_blocks, BN).transpose(1, 0, 2)
    vel_nodes = jnp.concatenate([vel_nodes, vel_nodes], axis=2)
    return jnp.pad(vel_nodes, ((0, 0), (0, ROWS - 3), (0, 0)))


def per_device(vort_p, pair_weights, pair_part, pair_node, counts):
    n_py, n_pz = lax.axis_size("py"), lax.axis_size("pz")
    node_blocks = NX * CY * CZ // BN
    sums, near = spread(vort_p, pair_weights, pair_part, pair_node, counts, node_blocks)
    x_modes = NX // 2
    devices = n_py * n_pz
    direct = devices <= 32 and x_modes % devices == 0 and x_modes // devices <= ROWS
    vel = (solve_direct if direct else solve_staged)(sums, n_py, n_pz)
    return collect(vel, near, pair_part, pair_node, counts)


def solution(mesh):
    placed = (
        P(None, ("py", "pz")),
        P(("py", "pz"), None, None),
        P(("py", "pz")),
        P(("py", "pz")),
        P(("py", "pz")),
    )
    return jax.shard_map(
        per_device, mesh=mesh, in_specs=placed, out_specs=P(None, ("py", "pz")), check_vma=False
    )
```

```python
import functools
import math

import jax
import jax.numpy as jnp
import numpy as np
from jax import lax
from jax.experimental import pallas as pl
from jax.experimental.pallas import tpu as pltpu
from jax.sharding import PartitionSpec as P

NX = 384
CY = 8
CZ = 2
BP = 128
BN = 64
PB_DEV = 32
ROWS = 8
CHUNK = 32
GROUP = 4
MESH = pl.DeviceIdType.MESH
f32 = jnp.float32
bf16 = jnp.bfloat16


def twiddle(row_index, col_index, period):
    product = row_index[:, None] * col_index[None, :] % period
    return product.astype(jnp.float32) * (2.0 * math.pi / period)


def forward_table(length):
    angle = twiddle(jnp.arange(length), jnp.arange(length), length)
    cosine = jnp.cos(angle)
    sines = jnp.sin(angle)
    return jnp.stack([jnp.stack([cosine, -sines], 1), jnp.stack([sines, cosine], 1)], 0)


def inverse_table(length):
    angle = twiddle(jnp.arange(length), jnp.arange(length), length)
    cosine = jnp.cos(angle) / length
    sines = jnp.sin(angle) / length
    return jnp.stack([jnp.stack([cosine, sines], 1), jnp.stack([-sines, cosine], 1)], 0)


def cross_terms(coeffs, field):
    return jnp.stack(
        [
            coeffs[1] * field[2] - coeffs[2] * field[1],
            coeffs[2] * field[0] - coeffs[0] * field[2],
            coeffs[0] * field[1] - coeffs[1] * field[0],
        ],
        axis=0,
    )


def signed_wave(length, index):
    signed = jnp.where(index < length // 2, index, index - length)
    return (signed.astype(jnp.float32) * (2.0 * math.pi / length), index == length // 2)


def curl_solve(spectrum, y_cells, z_cells):
    x_local = spectrum.shape[1]
    y_local = spectrum.shape[3]
    mode_x = lax.axis_index("py") * x_local + jnp.arange(x_local)
    wave_x = mode_x.astype(jnp.float32) * (2.0 * math.pi / NX)
    wave_y, edge_y = signed_wave(y_cells, lax.axis_index("pz") * y_local + jnp.arange(y_local))
    wave_z, edge_z = signed_wave(z_cells, jnp.arange(z_cells))
    wave_x3 = wave_x[:, None, None]
    wave_y3 = wave_y[None, :, None]
    wave_z3 = wave_z[None, None, :]
    total = wave_x3 * wave_x3 + wave_y3 * wave_y3 + wave_z3 * wave_z3
    edges = edge_y[None, :, None] | edge_z[None, None, :]
    keep = (total > 0) & jnp.logical_not(edges)
    inverse_sq = jnp.where(keep, 1.0 / jnp.where(keep, total, 1.0), 0.0)
    inv_wave = (wave_x3 * inverse_sq, wave_y3 * inverse_sq, wave_z3 * inverse_sq)
    real_turn = cross_terms(inv_wave, spectrum[:, :, 0])
    imag_turn = cross_terms(inv_wave, spectrum[:, :, 1])
    return jnp.stack([-imag_turn, real_turn], axis=2)


def halves(table):
    table = np.asarray(table, np.float32)
    high = table.astype(bf16)
    return high, (table - high.astype(np.float32)).astype(bf16)


def split(x):
    high = x.astype(bf16)
    return high, (x - high.astype(f32)).astype(bf16)


def dot(a, b, dims=((1,), (0,))):
    return lax.dot_general(a, b, (dims, ((), ())), preferred_element_type=f32)


def left_half(shape):
    return lax.broadcasted_iota(jnp.int32, shape, 1) < BN


def spread_kernel(part, node, count, parts_ref, w_ref, out_ref, near_ref, parts, sems):
    chunks = w_ref.shape[0] // CHUNK

    def fetch(k):
        here = pl.ds(k * CHUNK, CHUNK)
        return pltpu.make_async_copy(w_ref.at[here], near_ref.at[here], sems.at[k])

    for k in range(chunks):
        fetch(k).start()
    out_ref[...] = jnp.zeros_like(out_ref)
    parts[...] = jnp.zeros_like(parts)
    for b in range(PB_DEV):
        parts[b, 0:3, :] = parts_ref[:, b * BP : (b + 1) * BP].astype(f32)
    left = left_half((ROWS, 128))

    def chunk(k, carry):
        fetch(k).wait()
        base = k * CHUNK
        for g in range(CHUNK // GROUP):
            first = base + g * GROUP
            picked = jnp.concatenate([parts[part[first + i]] for i in range(GROUP)], axis=0)
            tiles = near_ref[pl.ds(first, GROUP)].reshape(GROUP * BN, BP)
            got = dot(picked.astype(bf16), tiles, ((1,), (1,)))
            for i in range(GROUP):
                keep = jnp.logical_and(left if i % 2 == 0 else ~left, first + i < count[0])
                lanes = i // 2 * 128
                own = got[i * ROWS : (i + 1) * ROWS, lanes : lanes + 128]
                out_ref[node[first + i]] += jnp.where(keep, own, 0.0)
        return carry

    lax.fori_loop(0, chunks, chunk, 0)


def spread(vort_p, weights, part, node, counts, node_blocks):
    smem = pl.BlockSpec(memory_space=pltpu.SMEM)
    vmem = pl.BlockSpec(memory_space=pltpu.VMEM)
    return pl.pallas_call(
        spread_kernel,
        out_shape=(
            jax.ShapeDtypeStruct((node_blocks, ROWS, 2 * BN), f32),
            jax.ShapeDtypeStruct(weights.shape, weights.dtype),
        ),
        in_specs=[smem, smem, smem, vmem, pl.BlockSpec(memory_space=pltpu.HBM)],
        out_specs=(vmem, vmem),
        scratch_shapes=[
            pltpu.VMEM((PB_DEV, ROWS, BP), f32),
            pltpu.SemaphoreType.DMA((weights.shape[0] // CHUNK,)),
        ],
        compiler_params=pltpu.CompilerParams(vmem_limit_bytes=48 * 2**20),
        name="spread",
    )(part, node, counts, vort_p, weights)


def collect_kernel(part, node, count, vel_ref, w_ref, out_ref, sums):
    sums[...] = jnp.zeros_like(sums)
    left = left_half((ROWS, 128))
    zero = jnp.zeros((ROWS, 128), f32)

    def chunk(k, carry):
        for g in range(CHUNK // GROUP):
            first = k * CHUNK + g * GROUP
            rows = []
            for i in range(GROUP):
                slot = first + i
                keep = jnp.logical_and(left if i % 2 == 0 else ~left, slot < count[0])
                own = jnp.where(keep, vel_ref[node[slot]], 0.0)
                rows.append(
                    jnp.concatenate(
                        [own if h == i // 2 else zero for h in range(GROUP // 2)], axis=1
                    )
                )
            chosen = jnp.concatenate(rows, axis=0).astype(bf16)
            got = dot(chosen, w_ref[pl.ds(first, GROUP)].reshape(GROUP * BN, BP))
            for i in range(GROUP):
                sums[part[first + i]] += got[i * ROWS : (i + 1) * ROWS]
        return carry

    lax.fori_loop(0, w_ref.shape[0] // CHUNK, chunk, 0)
    for b in range(PB_DEV):
        out_ref[:, b * BP : (b + 1) * BP] = sums[b, 0:3, :]


def collect(vel, weights, part, node, counts):
    smem = pl.BlockSpec(memory_space=pltpu.SMEM)
    vmem = pl.BlockSpec(memory_space=pltpu.VMEM)
    return pl.pallas_call(
        collect_kernel,
        out_shape=jax.ShapeDtypeStruct((3, PB_DEV * BP), f32),
        in_specs=[smem, smem, smem, vmem, vmem],
        out_specs=vmem,
        scratch_shapes=[pltpu.VMEM((PB_DEV, ROWS, BP), f32)],
        compiler_params=pltpu.CompilerParams(vmem_limit_bytes=24 * 2**20),
        name="collect",
    )(part, node, counts, vel, weights)


def tables(n_py, n_pz):
    devices = n_py * n_pz
    local = NX // 2 // devices
    ny, nz = CY * n_py, CZ * n_pz
    row = np.arange(devices * ROWS)
    slot, device = row % ROWS, row // ROWS
    mode = device * local + slot
    angle = 2 * np.pi * (mode[:, None] * np.arange(NX)[None] % NX) / NX
    used = (slot < local)[:, None]
    x_cos, x_sin = np.where(used, np.cos(angle), 0.0), np.where(used, -np.sin(angle), 0.0)
    index = np.arange(devices)
    a, b = index // n_pz, index % n_pz
    theta = 2 * np.pi * (a[:, None] * a[None] / n_py + b[:, None] * b[None] / n_pz)
    eye = np.eye(ROWS)
    far = np.concatenate([np.kron(np.cos(theta), eye), np.kron(np.sin(theta), eye)], 0)
    lane = np.arange(128)
    real, comp, cell = lane // 64, lane % 64 // 16, lane % 16
    zl, yl = cell // CY, cell % CY
    valid = (comp < 3)[None]
    phi = 2 * np.pi * (a[:, None] * yl[None] / ny + b[:, None] * zl[None] / nz)
    sign = np.where(real == 0, 1.0, -1.0)[None]
    turn_cos, turn_sin = np.cos(phi), np.sin(phi) * sign
    psi = 2 * np.pi * (yl[:, None] * yl[None] / CY + zl[:, None] * zl[None] / CZ)

    def near(ahead):
        cosine, sines = np.cos(psi), np.sin(psi)
        r, q = real[:, None], real[None]
        both = np.where(r == q, sines, np.where(r == 0, cosine, -cosine))
        same = (comp[:, None] == (comp[None] + ahead) % 3) & (comp[:, None] < 3) & valid
        return np.where(same, both, 0.0)

    forward = np.concatenate([near(2), near(1)], 1)
    cosine, sines = np.cos(psi), np.sin(psi)
    r, q = real[:, None], real[None]
    both = np.where(r == q, cosine, np.where(r == 0, sines, -sines))
    same = (comp[:, None] == comp[None]) & (comp[:, None] < 3)
    back = np.where(same, both, 0.0)
    my, mz = a[:, None] + n_py * yl[None], b[:, None] + n_pz * zl[None]
    keep = (my != ny // 2) & (mz != nz // 2) & valid
    my, mz = np.where(my < ny // 2, my, my - ny), np.where(mz < nz // 2, mz, mz - nz)
    ky, kz = 2 * np.pi * my / ny, 2 * np.pi * mz / nz
    zero = np.zeros_like(ky)
    wave = np.stack([zero, ky, kz])
    k_first = np.where(comp == 0, wave[1], np.where(comp == 1, wave[2], wave[0]))
    k_second = np.where(comp == 0, wave[2], np.where(comp == 1, wave[0], wave[1]))
    x_first = np.broadcast_to(comp == 2, ky.shape)
    x_second = np.broadcast_to(comp == 1, ky.shape)
    small = [turn_cos, turn_sin, ky * ky + kz * kz, k_first, k_second, x_first, x_second, keep]
    small = np.stack(small).astype(np.float32)
    return [
        *halves(np.stack([x_cos, x_sin])),
        *halves(far),
        *halves(forward),
        *halves(back),
        small,
    ]


def solve_kernel(
    n_py,
    n_pz,
    count,
    part_ref,
    node_ref,
    parts_ref,
    w_ref,
    *rest_refs,
):
    n_consts = 9
    consts, out_ref = rest_refs[:n_consts], rest_refs[n_consts]
    held = rest_refs[n_consts + 1 : 2 * n_consts + 1]
    (
        near_ref,
        vel_ref,
        send_a,
        recv_a,
        send_b,
        recv_b,
        send_sem,
        recv_sem,
        parts,
        picks,
        pairs,
        sems,
        const_sems,
    ) = rest_refs[2 * n_consts + 1 :]
    xh_ref, xl_ref, far_h, far_l, fwd_h, fwd_l, back_h, back_l, small = held
    devices = n_py * n_pz
    local = NX // 2 // devices
    rows = devices * ROWS
    per_row = NX // BN
    cells = CY * CZ
    my_y, my_z = lax.axis_index("py"), lax.axis_index("pz")
    me = my_y * n_pz + my_z
    slots = w_ref.shape[0]
    chunks = slots // CHUNK
    barrier = pltpu.get_barrier_semaphore()

    def fetch(k):
        here = pl.ds(k * CHUNK, CHUNK)
        return pltpu.make_async_copy(w_ref.at[here], near_ref.at[here], sems.at[k])

    for k in range(chunks):
        fetch(k).start()
    loads = [
        pltpu.make_async_copy(c, h, const_sems.at[i]) for i, (c, h) in enumerate(zip(consts, held))
    ]
    for load in loads:
        load.start()
    vel_ref[...] = jnp.zeros_like(vel_ref)
    recv_a[...] = jnp.zeros_like(recv_a)
    recv_b[...] = jnp.zeros_like(recv_b)

    def greet(k, carry):
        other = lax.rem(me + k, devices)
        pl.semaphore_signal(
            barrier, inc=1, device_id=(other // n_pz, lax.rem(other, n_pz)), device_id_type=MESH
        )
        return carry

    lax.fori_loop(1, devices, greet, 0)

    sent = pl.ds(0, local)

    def exchange(send, recv, phase):
        order = list(range(1, devices))
        turns = [lax.rem(my_y + k, n_py) for k in range(n_py)]
        if n_py == 4:
            order = list(range(devices - n_pz)) + list(range(devices - n_pz + 1, devices))
            turns = [3 - my_y, turns[2], 3 - turns[2], my_y]
        for k in order:
            to_y = turns[k // n_pz]
            to_z = lax.rem(my_z + k % n_pz, n_pz)
            pltpu.make_async_remote_copy(
                src_ref=send.at[to_y * n_pz + to_z, sent],
                dst_ref=recv.at[me, sent],
                send_sem=send_sem.at[phase],
                recv_sem=recv_sem.at[phase],
                device_id=(to_y, to_z),
                device_id_type=MESH,
            ).start()

    def finish(send, recv, phase):
        many = pl.ds(0, devices - 1)
        pltpu.make_async_copy(recv.at[many, sent], recv.at[many, sent], recv_sem.at[phase]).wait()

    def drain(send, phase):
        many = pl.ds(0, devices - 1)
        pltpu.make_async_copy(send.at[many, sent], send.at[many, sent], send_sem.at[phase]).wait()

    picks[...] = jnp.zeros_like(picks)
    parts[...] = jnp.zeros_like(parts)
    for b in range(PB_DEV):
        parts[b * ROWS : b * ROWS + 3, :] = parts_ref[:, b * BP : (b + 1) * BP].astype(f32)
    row = lax.broadcasted_iota(jnp.int32, (PB_DEV, slots), 0)
    chooser = jnp.where(row == part_ref[...], 1.0, 0.0).T.astype(bf16)
    for c in range(3):
        block = parts[pl.ds(c, PB_DEV, stride=ROWS), :].astype(bf16)
        picks[pl.ds(c, slots, stride=ROWS), :] = dot(chooser, block)
    near_half = left_half((ROWS, 128))

    def chunk(k, carry):
        fetch(k).wait()
        for g in range(CHUNK // GROUP):
            first = k * CHUNK + g * GROUP
            picked = picks[pl.ds(first * ROWS, GROUP * ROWS), :]
            tiles = near_ref[pl.ds(first, GROUP)].reshape(GROUP * BN, BP)
            got = dot(picked.astype(bf16), tiles, ((1,), (1,)))
            own = []
            for i in range(GROUP):
                lanes = i // 2 * 128
                keep = near_half if i % 2 == 0 else ~near_half
                piece = got[i * ROWS : (i + 1) * ROWS, lanes : lanes + 128]
                own.append(jnp.where(keep, piece, 0.0))
            pairs[pl.ds(first * ROWS, GROUP * ROWS), :] = jnp.concatenate(own, axis=0)
        return carry

    lax.fori_loop(0, chunks, chunk, 0)
    for load in loads:
        load.wait()
    row = lax.broadcasted_iota(jnp.int32, (cells * per_row, slots), 0)
    block = row % cells * per_row + row // cells
    live = lax.broadcasted_iota(jnp.int32, (cells * per_row, slots), 1) < count[0]
    hits = jnp.where((block == node_ref[...]) & live, 1.0, 0.0).astype(bf16)
    left = left_half((cells, 128))
    lines = []
    for c in range(3):
        high, rest = split(pairs[pl.ds(c, slots, stride=ROWS), :])
        total = dot(hits, high) + dot(hits, rest)
        total += pltpu.roll(total, BN, 1)
        pieces = [
            jnp.where(
                left, total[xb * cells : (xb + 1) * cells], total[(xb + 1) * cells : (xb + 2) * cells]
            )
            for xb in range(0, per_row, 2)
        ]
        lines.append(jnp.concatenate(pieces, axis=1))
    vort = jnp.concatenate(lines, axis=0)
    low = jnp.concatenate([vort, jnp.zeros((80, NX), f32)], axis=0)
    up = jnp.concatenate([jnp.zeros((64, NX), f32), vort, jnp.zeros((16, NX), f32)], axis=0)
    over = ((1,), (1,))
    modes = jnp.zeros((rows, 128), f32)
    for k, field in ((0, low), (1, up)):
        high, rest = split(field)
        modes += dot(xh_ref[k], high, over) + (
            dot(xh_ref[k], rest, over) + dot(xl_ref[k], high, over)
        )
    send_a[...] = modes.reshape(devices, ROWS, 128)
    recv_a[me] = send_a[me]
    pl.semaphore_wait(barrier, devices - 1)
    exchange(send_a, recv_a, 0)

    def spread_out(i):
        return jnp.broadcast_to(small[i][:, None, :], (devices, ROWS, 128)).reshape(rows, 128)

    slot = lax.broadcasted_iota(jnp.int32, (rows, 128), 0) % ROWS
    mode = me * local + slot
    wave_x = mode.astype(f32) * (2.0 * math.pi / NX)
    total = spread_out(2) + wave_x * wave_x
    ny_nz = CY * n_py * CZ * n_pz
    weight = jnp.where(mode == 0, 1.0, 2.0) * (1.0 / (NX * ny_nz))
    inverse = spread_out(7) * weight / jnp.where(total > 0, total, 1.0)
    gain_a = (spread_out(3) + wave_x * spread_out(5)) * inverse
    gain_b = (spread_out(4) + wave_x * spread_out(6)) * inverse
    turn_cos, turn_sin = spread_out(0), spread_out(1)
    sign = jnp.where(lax.broadcasted_iota(jnp.int32, (rows, 128), 1) < 64, 1.0, -1.0)

    def swap(x):
        return pltpu.roll(x, 64, 1)

    def across(x):
        high, rest = split(x)
        both = dot(far_h[...], high) + (dot(far_h[...], rest) + dot(far_l[...], high))
        return both[:rows], swap(both[rows:]) * sign

    def along(x, table_h, table_l):
        high, rest = split(x)
        return dot(high, table_h[...]) + (dot(rest, table_h[...]) + dot(high, table_l[...]))

    finish(send_a, recv_a, 0)
    even, odd = across(recv_a[...].reshape(rows, 128))
    y = even + odd
    z = turn_cos * y + turn_sin * swap(y)
    both = along(z, fwd_h, fwd_l)
    vel = gain_a * both[:, :128] - gain_b * both[:, 128:]
    y = along(vel, back_h, back_l)
    z = turn_cos * y - turn_sin * swap(y)
    even, odd = across(z)
    send_b[...] = (even - odd).reshape(devices, ROWS, 128)
    recv_b[me] = send_b[me]
    exchange(send_b, recv_b, 1)
    drain(send_a, 0)
    finish(send_b, recv_b, 1)
    back = recv_b[...].reshape(rows, 128).T
    grid = jnp.zeros((48, NX), f32)
    for k in range(2):
        high, rest = split(back[64 * k : 64 * k + 48])
        grid += dot(high, xh_ref[k]) + (dot(rest, xh_ref[k]) + dot(high, xl_ref[k]))
    grid = grid.astype(bf16).astype(f32)
    for c in range(3):
        for xb in range(0, per_row, 2):
            piece = grid[c * cells : (c + 1) * cells, xb * BN : (xb + 2) * BN]
            other = pltpu.roll(piece, BN, 1)
            for h, both in ((0, jnp.where(left, piece, other)), (1, jnp.where(left, other, piece))):
                where = pl.ds((xb + h) * ROWS + c, cells, stride=per_row * ROWS)
                vel_ref[where, :] = both

    row = lax.broadcasted_iota(jnp.int32, (cells * per_row, slots), 0)
    chooser = jnp.where(row == node_ref[...], 1.0, 0.0).T.astype(bf16)
    for c in range(3):
        block = vel_ref[pl.ds(c, cells * per_row, stride=ROWS), :].astype(bf16)
        picks[pl.ds(c, slots, stride=ROWS), :] = dot(chooser, block)

    def gather(k, carry):
        for g in range(CHUNK // GROUP):
            first = k * CHUNK + g * GROUP
            lines = []
            for i in range(GROUP):
                keep = near_half if i % 2 == 0 else ~near_half
                own = jnp.where(keep, picks[pl.ds((first + i) * ROWS, ROWS), :], 0.0)
                zero = jnp.zeros((ROWS, 128), f32)
                lines.append(
                    jnp.concatenate(
                        [own if h == i // 2 else zero for h in range(GROUP // 2)], axis=1
                    )
                )
            chosen = jnp.concatenate(lines, axis=0).astype(bf16)
            tiles = near_ref[pl.ds(first, GROUP)].reshape(GROUP * BN, BP)
            pairs[pl.ds(first * ROWS, GROUP * ROWS), :] = dot(chosen, tiles)
        return carry

    lax.fori_loop(0, chunks, gather, 0)
    row = lax.broadcasted_iota(jnp.int32, (PB_DEV, slots), 0)
    live = lax.broadcasted_iota(jnp.int32, (PB_DEV, slots), 1) < count[0]
    hits = jnp.where((row == part_ref[...]) & live, 1.0, 0.0).astype(bf16)
    for c in range(3):
        high, rest = split(pairs[pl.ds(c, slots, stride=ROWS), :])
        out_ref[c] = dot(hits, high) + dot(hits, rest)
    drain(send_b, 1)


def solve_direct(vort_p, weights, part, node, counts, n_py, n_pz):
    devices = n_py * n_pz
    node_blocks = NX * CY * CZ // BN
    slots = weights.shape[0]
    smem = pl.BlockSpec(memory_space=pltpu.SMEM)
    vmem = pl.BlockSpec(memory_space=pltpu.VMEM)
    hbm = pl.BlockSpec(memory_space=pltpu.HBM)
    block = pltpu.VMEM((devices, ROWS, 128), f32)
    consts = tables(n_py, n_pz)
    consts = [jnp.asarray(t) for t in consts]
    out = pl.pallas_call(
        functools.partial(solve_kernel, n_py, n_pz),
        out_shape=jax.ShapeDtypeStruct((3, PB_DEV, BP), f32),
        in_specs=[smem, vmem, vmem, vmem, hbm] + [hbm] * len(consts),
        out_specs=vmem,
        scratch_shapes=[
            *[pltpu.VMEM(t.shape, t.dtype) for t in consts],
            pltpu.VMEM(weights.shape, weights.dtype),
            pltpu.VMEM((node_blocks * ROWS, 2 * BN), f32),
            block,
            block,
            block,
            block,
            pltpu.SemaphoreType.DMA((2,)),
            pltpu.SemaphoreType.DMA((2,)),
            pltpu.VMEM((PB_DEV * ROWS, BP), f32),
            pltpu.VMEM((slots * ROWS, 128), f32),
            pltpu.VMEM((slots * ROWS, 128), f32),
            pltpu.SemaphoreType.DMA((slots // CHUNK,)),
            pltpu.SemaphoreType.DMA((len(consts),)),
        ],
        compiler_params=pltpu.CompilerParams(
            collective_id=0, has_side_effects=True, vmem_limit_bytes=60 * 2**20
        ),
        name="solve",
    )(counts, part[None], node[None], vort_p, weights, *consts)
    return out.reshape(3, PB_DEV * BP)


def solve_staged(sums, n_py, n_pz):
    highest = lax.Precision.HIGHEST
    node_blocks = sums.shape[0]
    y_cells, z_cells = CY * n_py, CZ * n_pz
    x_modes = NX // 2
    sums = sums[:, :3, :BN] + sums[:, :3, BN:]
    vort_grid = sums.transpose(1, 0, 2).reshape(3, CZ, CY, NX)
    angle_fwd = twiddle(jnp.arange(NX), jnp.arange(x_modes), NX)
    x_forward = jnp.stack([jnp.cos(angle_fwd), -jnp.sin(angle_fwd)], 1)
    angle_inv = twiddle(jnp.arange(x_modes), jnp.arange(NX), NX)
    mode_weight = (jnp.where(jnp.arange(x_modes) == 0, 1.0, 2.0) / NX)[:, None]
    x_inverse = jnp.stack([mode_weight * jnp.cos(angle_inv), -mode_weight * jnp.sin(angle_inv)], 0)
    y_forward = forward_table(y_cells)
    z_forward = forward_table(z_cells)
    z_inverse = inverse_table(z_cells)
    y_inverse = inverse_table(y_cells)
    x_spectrum = jnp.einsum("czyx,xrm->czrmy", vort_grid, x_forward, precision=highest)
    row_section = jnp.einsum(
        "czrmy,rysk->cmskz",
        lax.all_to_all(x_spectrum, "py", split_axis=3, concat_axis=4, tiled=True),
        y_forward,
        precision=highest,
    )
    col_section = jnp.einsum(
        "cmrkz,rzsw->cmskw",
        lax.all_to_all(row_section, "pz", split_axis=3, concat_axis=4, tiled=True),
        z_forward,
        precision=highest,
    )
    vel_spectrum = curl_solve(col_section, y_cells, z_cells)
    z_back = jnp.einsum("cmrkw,rwsz->cmszk", vel_spectrum, z_inverse, precision=highest)
    y_back = jnp.einsum(
        "cmrzk,rksy->czsym",
        lax.all_to_all(z_back, "pz", split_axis=3, concat_axis=4, tiled=True),
        y_inverse,
        precision=highest,
    )
    vel_grid = jnp.einsum(
        "czrym,rmx->czyx",
        lax.all_to_all(y_back, "py", split_axis=3, concat_axis=4, tiled=True),
        x_inverse,
        precision=highest,
    )
    vel_nodes = vel_grid.astype(bf16).astype(f32).reshape(3, node_blocks, BN).transpose(1, 0, 2)
    vel_nodes = jnp.concatenate([vel_nodes, vel_nodes], axis=2)
    return jnp.pad(vel_nodes, ((0, 0), (0, ROWS - 3), (0, 0)))


def per_device(vort_p, pair_weights, pair_part, pair_node, counts):
    n_py, n_pz = lax.axis_size("py"), lax.axis_size("pz")
    node_blocks = NX * CY * CZ // BN
    devices, x_modes = n_py * n_pz, NX // 2
    if devices <= 32 and x_modes % devices == 0 and x_modes // devices <= ROWS:
        return solve_direct(vort_p, pair_weights, pair_part, pair_node, counts, n_py, n_pz)
    sums, near = spread(vort_p, pair_weights, pair_part, pair_node, counts, node_blocks)
    vel = solve_staged(sums, n_py, n_pz)
    return collect(vel, near, pair_part, pair_node, counts)


def solution(mesh):
    placed = (
        P(None, ("py", "pz")),
        P(("py", "pz"), None, None),
        P(("py", "pz")),
        P(("py", "pz")),
        P(("py", "pz")),
    )
    return jax.shard_map(
        per_device, mesh=mesh, in_specs=placed, out_specs=P(None, ("py", "pz")), check_vma=False
    )
```
